128 devices in a mesh: segment: 4 (over z), tok: 32 (over y, x, core).
Axes of the slice: x: 4, y: 4, z: 4, core: 2. Of those that a mesh axis runs over, the one named last changes fastest.
Arguments:
- acts: bfloat16 [4, 4096, 8192], P('segment', 'tok'), may hold values from -6 to 6
- output_gradient: bfloat16 [4, 4096, 1024], P('segment', 'tok'), may hold values from -6 to 6
- frozen: bfloat16 [4, 8192, 1024], P('segment', 'tok'), may hold values from -0.0625 to 0.0625
- adapter_down: bfloat16 [4, 128, 64, 8192], P('segment', 'tok'), may hold values from -0.0625 to 0.0625
- adapter_up: bfloat16 [4, 128, 64, 1024], P('segment', 'tok'), may hold values from -0.1875 to 0.1875
- assign: int32 [4, 4096], P('segment', 'tok'), may hold values from 0 to 127, as said below
- adapter_slot: int32 [128], replicated, may hold values from 0 to 127, as said below
Outputs:
- passed: bfloat16 [4, 4096, 8192], P('segment', 'tok')
- down_gradient: float32 [4, 128, 64, 8192], P('segment', 'tok')
- up_gradient: float32 [4, 128, 64, 1024], P('segment', 'tok')
The draws below stay inside these ranges and needn't reach their ends.
Inputs may be any that keep to these rules, and one draw needn't show every extreme that they name: A permutation of the slots: adapter a is held in slot adapter_slot[a], on device adapter_slot[a] // 4 of tok. `assign`: the 128 tokens of one device are sorted by adapter. Of one device's tokens at most 10 have adapters held by any one device of tok; in every section some device of tok holds the adapters of exactly 10 tokens of every device.
All inputs are finite; a program needn't handle non-finite values.
Results may differ from the reference program's by a relative error of at most 0.012.
Values may be sent and summed in bfloat16 or wider, within the bound.
A program may use at most 128 MiB of HBM per device.

```python
import math
import jax
import jax.numpy as jnp
from jax import lax

MODEL_DIMENSION = 8192
VALUE_WIDTH = 1024
ADAPTER_RANK = 64
ADP_DEV = 4
TOK_DEV = 128
SECTION_TOKENS = 4096
ADAPTER_TOTAL = 128
CAP = 10
N_SEGMENT = 4
N_TOK = 32


def adapter_slots(key):
    return jax.random.permutation(jax.random.fold_in(key, 11), ADAPTER_TOTAL).astype(jnp.int32)


def draw_adapter_slot(key, part):
    shared = adapter_slots(key)
    return shared


def draw_assign(key, part):
    shared = adapter_slots(key)
    key = jax.random.fold_in(key, 5)
    adapter_at = jnp.argsort(shared, stable=True).astype(jnp.int32)
    hot_key, rest_key, pick_key = jax.random.split(key, 3)
    hottest = jax.random.randint(hot_key, (N_SEGMENT, 1, 1), 0, N_TOK).astype(jnp.int32)
    block_keys = jax.random.split(rest_key, N_SEGMENT * N_TOK)
    others = jax.vmap(lambda k: jax.random.permutation(k, N_TOK - 1))(block_keys)
    others = others.reshape(N_SEGMENT, N_TOK, N_TOK - 1).astype(jnp.int32)
    row_ids = jnp.arange(TOK_DEV, dtype=jnp.int32)
    ranked = jnp.where(row_ids < CAP, 0, 1 + (row_ids - CAP) % (N_TOK - 1))
    other_pick = jnp.take_along_axis(others, jnp.broadcast_to(jnp.maximum(ranked - 1, 0), (N_SEGMENT, N_TOK, TOK_DEV)), axis=2)
    owner_of = jnp.where(ranked[None, None, :] == 0, hottest, (hottest + 1 + other_pick) % N_TOK)
    within = jax.random.randint(pick_key, (N_SEGMENT, N_TOK, TOK_DEV), 0, ADP_DEV).astype(jnp.int32)
    chosen = adapter_at[owner_of * ADP_DEV + within]
    chosen = jnp.sort(chosen, axis=-1)
    return chosen.reshape(N_SEGMENT, SECTION_TOKENS).astype(jnp.int32)


def shard_levels(own_key, shape, pieces, least, top_value):
    level, own = 1.0, jax.random.fold_in(own_key, 6)
    for axis_at, shards_of in pieces:
        heights = jnp.exp(jax.random.uniform(jax.random.fold_in(own, axis_at), (shards_of,), jnp.float32, least / len(pieces), top_value / len(pieces)))
        level = level * jnp.repeat(heights, shape[axis_at] // shards_of).reshape([-1 if axis == axis_at else 1 for axis in range(len(shape))])
    return level


def gaussian(key, extent, deviation, bound, pieces=(), kind=jnp.bfloat16):
    drawn = jax.random.normal(key, extent, jnp.float32) * deviation
    if len(pieces) > 0:
        drawn = shard_levels(key, extent, pieces, -0.22, 0.18) * drawn
    return jnp.clip(drawn, min=-bound, max=bound).astype(kind)


def setup_inputs(seed: int = 0) -> dict:
    keys = jax.random.split(jax.random.key(seed), 8)
    return {
        "acts": gaussian(keys[0], (N_SEGMENT, SECTION_TOKENS, MODEL_DIMENSION), 1.0, 6.0, ((0, 4), (1, 32))),
        "output_gradient": gaussian(keys[1], (N_SEGMENT, SECTION_TOKENS, VALUE_WIDTH), 1.0, 6.0, ((0, 4), (1, 32))),
        "frozen": gaussian(keys[2], (N_SEGMENT, MODEL_DIMENSION, VALUE_WIDTH), MODEL_DIMENSION ** -0.5, 0.0625, ((0, 4), (1, 32))),
        "adapter_down": gaussian(keys[3], (N_SEGMENT, ADAPTER_TOTAL, ADAPTER_RANK, MODEL_DIMENSION), MODEL_DIMENSION ** -0.5, 0.0625, ((0, 4), (1, 32))),
        "adapter_up": gaussian(keys[4], (N_SEGMENT, ADAPTER_TOTAL, ADAPTER_RANK, VALUE_WIDTH), VALUE_WIDTH ** -0.5, 0.1875, ((0, 4), (1, 32))),
        "assign": draw_assign(jax.random.fold_in(keys[7], 71), 0),
        "adapter_slot": draw_adapter_slot(jax.random.fold_in(keys[7], 71), 0),
    }


adapter_scale = 2.0


def section_backward(inputs, out_grads, weight, down_mats, up_mats, slot_position):
    frozen_piece = jnp.dot(out_grads, weight.T, preferred_element_type=jnp.float32).astype(jnp.bfloat16)
    block_rows = math.gcd(SECTION_TOKENS, 32)
    blocks = SECTION_TOKENS // block_rows
    xs = (inputs.reshape(blocks, block_rows, MODEL_DIMENSION), out_grads.reshape(blocks, block_rows, VALUE_WIDTH),
          slot_position.reshape(blocks, block_rows).astype(jnp.int32))

    def step(carry, block):
        acc_a, accumulated_up = carry
        in_blk, grad_blk, index_block = block
        mats_a = down_mats[index_block].astype(jnp.float32)
        up_matrices = up_mats[index_block].astype(jnp.float32)
        in_f = in_blk.astype(jnp.float32)
        frozen_gradient = grad_blk.astype(jnp.float32)
        low = jnp.einsum('trd,td->tr', mats_a, in_f).astype(jnp.bfloat16)
        lifted_rows = (adapter_scale * jnp.einsum('yzd,yd->yz', up_matrices, frozen_gradient)).astype(jnp.bfloat16)
        lifted_f = lifted_rows.astype(jnp.float32)
        reduced_frozen = low.astype(jnp.float32)
        part = jnp.einsum('tr,trd->td', lifted_f, mats_a).astype(jnp.bfloat16)
        acc_a = acc_a.at[index_block].add(jnp.einsum('tr,td->trd', lifted_f, in_f))
        accumulated_up = accumulated_up.at[index_block].add(adapter_scale * jnp.einsum('wu,wc->wuc', reduced_frozen, frozen_gradient))
        return (acc_a, accumulated_up), part

    init = (jnp.zeros((ADAPTER_TOTAL, ADAPTER_RANK, MODEL_DIMENSION), jnp.float32), jnp.zeros((ADAPTER_TOTAL, ADAPTER_RANK, VALUE_WIDTH), jnp.float32))
    (acc_a, accumulated_up), section_parts = lax.scan(step, init, xs)
    adapter_piece = section_parts.reshape(SECTION_TOKENS, MODEL_DIMENSION)
    summed_rows = (frozen_piece.astype(jnp.float32) + adapter_piece.astype(jnp.float32)).astype(jnp.bfloat16)
    return summed_rows, acc_a, accumulated_up


def reference(acts, output_gradient, frozen, adapter_down, adapter_up, assign, adapter_slot):
    passes = []
    grads_a = []
    grads_b = []
    for section_number in range(N_SEGMENT):
        slot_position = adapter_slot[assign[section_number]].astype(jnp.int32)
        summed_rows, acc_a, accumulated_up = section_backward(acts[section_number], output_gradient[section_number], frozen[section_number],
                                                adapter_down[section_number], adapter_up[section_number], slot_position)
        passes.append(summed_rows)
        grads_a.append(acc_a)
        grads_b.append(accumulated_up)
    passed = jnp.roll(jnp.stack(passes), -1, axis=0)
    return passed, jnp.stack(grads_a), jnp.stack(grads_b)
```

```python
import functools

import jax
import jax.numpy as jnp
from jax import lax
from jax.experimental import pallas as pl
from jax.experimental.pallas import tpu as pltpu
from jax.sharding import PartitionSpec as P

MESH = pl.DeviceIdType.MESH
BF16 = jnp.bfloat16
F32 = jnp.float32
ADAPTER_SCALE = 2.0

TOKENS = 128
WIDTH = 8192
VALUE = 1024
RANK_ROWS = 256
OWNERS = 32
CAP = 10
SLICES = 8
SLICE = WIDTH // SLICES
PIECE = 16
CHUNKS = SLICES * CAP // PIECE
ROWS = OWNERS * PIECE
TILE = 256
MARK = 128
NX = 4


def slices_of(chunk):
    first, last = chunk * PIECE // CAP, (chunk * PIECE + PIECE - 1) // CAP
    return list(range(first, last + 1))


def first_chunk(j):
    return j * CAP // PIECE


def last_chunk(j):
    return (j * CAP + CAP - 1) // PIECE


def iota(shape, axis):
    return lax.broadcasted_iota(jnp.int32, shape, axis)


def dot(a, b, precision=None):
    return lax.dot_general(a, b, (((1,), (0,)), ((), ())), precision=precision, preferred_element_type=F32)


def dot_t(a, b):
    return lax.dot_general(a, b, (((1,), (1,)), ((), ())), preferred_element_type=F32)


def one_hot(flag):
    return jnp.where(flag, 1.0, 0.0).astype(BF16)


def pick(chunk, j, axis, dest):
    shape = (ROWS, TOKENS) if axis == 0 else (TOKENS, ROWS)
    row = iota(shape, axis)
    rank = (row & 15) + (PIECE * chunk - CAP * j)
    target = (row >> 4) * CAP + rank
    return one_hot((dest == target) & (rank >= 0) & (rank < CAP))


def spread(chunk, js, axis):
    shape = (128, 128)
    row, col = iota(shape, axis), iota(shape, 1 - axis)
    out = None
    for j in js:
        rank = (row & 15) + (PIECE * chunk - CAP * j)
        flag = ((row >> 4) == (col >> 4)) & ((col & 15) == rank) & (rank >= 0) & (rank < CAP)
        out = flag if out is None else out | flag
    return jnp.where(out, 1.0, 0.0)


def kernel(
    acts, grads, frozen, down, up, assign, slots,
    passed, down_grad, up_grad,
    acts_v, grads_v, down_v, up_v, dest_row, dest_col,
    gs, gr, fs, fr, rs, rr, gx, wy, ft, fp,
    lift_src, lift_t, mask_t, lift_q, liftt_q, low_q, low_t, pend, fin, dg, ug,
    in_sem, g_sem, f_send, f_recv, r_send, r_recv, gx_sem, wy_sem, fp_sem, z_send, z_recv, dg_sem, ug_sem,
):
    seg = lax.axis_index("segment")
    me = lax.axis_index("tok")
    y, x, core = me // 8, (me // 2) % 4, me % 2
    col8 = me % 8
    before, after = (seg + 3) % 4, (seg + 1) % 4

    loads = [
        pltpu.make_async_copy(grads, grads_v, in_sem.at[0]),
        pltpu.make_async_copy(acts, acts_v, in_sem.at[1]),
        pltpu.make_async_copy(up, up_v, in_sem.at[2]),
        pltpu.make_async_copy(down, down_v, in_sem.at[3]),
        pltpu.make_async_copy(frozen, wy.at[y], in_sem.at[4]),
        pltpu.make_async_copy(grads, gx.at[col8], in_sem.at[5]),
    ]
    for load in loads:
        load.start()

    barrier = pltpu.get_barrier_semaphore()

    def greet(k, carry):
        pl.semaphore_signal(barrier, inc=1, device_id=(seg, (me + k) % OWNERS), device_id_type=MESH)
        return carry

    lax.fori_loop(1, OWNERS, greet, 0)
    pl.semaphore_signal(barrier, inc=1, device_id=(after, me), device_id_type=MESH)

    match = one_hot(assign[...] == iota((128, 128), 0))
    slot = dot(jnp.broadcast_to(slots[...], (16, 128)).astype(F32).astype(BF16), match)[0:1].astype(jnp.int32)
    owner, local = slot >> 2, slot & 3
    hot = jnp.where(owner == iota((OWNERS, TOKENS), 0), 1.0, 0.0)
    earlier = one_hot(iota((TOKENS, TOKENS), 0) < iota((TOKENS, TOKENS), 1))
    rank = jnp.sum(hot * dot(hot.astype(BF16), earlier), axis=0, keepdims=True)
    dest = owner * CAP + rank.astype(jnp.int32)
    dest_row[...] = jnp.broadcast_to(dest, (8, TOKENS))
    dest_col[...] = jnp.transpose(jnp.broadcast_to(dest.astype(F32), (TOKENS, TOKENS))).astype(jnp.int32)

    local_hot = one_hot(local == iota((MARK, TOKENS), 0))
    row = iota((ROWS, TOKENS), 0)
    chosen = one_hot((dest == (row >> 4) * CAP + (row & 15)) & ((row & 15) < CAP))
    gs[:, VALUE:] = dot_t(chosen, local_hot).astype(BF16)
    loads[0].wait()
    for c0 in range(0, VALUE, TILE):
        gs[:, c0 : c0 + TILE] = dot(chosen, grads_v[:, c0 : c0 + TILE]).astype(BF16)

    def piece(owner_at):
        return pl.ds(pl.multiple_of(owner_at * PIECE, PIECE), PIECE)

    def send_pieces(src, dst, send_sem, recv_sem):
        def one(k, carry):
            to = (me + k) % OWNERS
            pltpu.make_async_remote_copy(
                src_ref=src.at[piece(to)],
                dst_ref=dst.at[piece(me)],
                send_sem=send_sem,
                recv_sem=recv_sem,
                device_id=(seg, to),
                device_id_type=MESH,
            ).start()
            return carry

        lax.fori_loop(1, OWNERS, one, 0)
        dst[piece(me)] = src[piece(me)]

    def wait_pieces(buf, sem):
        others = buf.at[pl.ds(0, ROWS - PIECE)]
        pltpu.make_async_copy(others, others, sem).wait()

    pl.semaphore_wait(barrier, OWNERS)
    send_pieces(gs, gr, g_sem.at[0], g_sem.at[1])

    def send_frozen(k, carry):
        to = ((y + k) % 4) * 8 + col8
        pltpu.make_async_remote_copy(
            src_ref=frozen, dst_ref=wy.at[y], send_sem=wy_sem.at[0], recv_sem=wy_sem.at[1],
            device_id=(seg, to), device_id_type=MESH,
        ).start()
        return carry

    def send_grads(k, carry):
        to = y * 8 + (col8 + k) % 8
        pltpu.make_async_remote_copy(
            src_ref=grads, dst_ref=gx.at[col8], send_sem=gx_sem.at[0], recv_sem=gx_sem.at[1],
            device_id=(seg, to), device_id_type=MESH,
        ).start()
        return carry

    lax.fori_loop(1, 4, send_frozen, 0)
    lax.fori_loop(1, 8, send_grads, 0)

    def send_acts(q):
        src = fs.at[q]

        def step(ct, carry):
            cols = pl.ds(pl.multiple_of(ct * TILE, TILE), TILE)
            total = None
            for j in slices_of(q):
                mine = pl.ds(pl.multiple_of(j * SLICE + ct * TILE, TILE), TILE)
                term = dot(pick(q, j, 0, dest_row[0:1]), acts_v[:, mine])
                total = term if total is None else total + term
            src[:, cols] = total.astype(BF16)
            return carry

        lax.fori_loop(0, SLICE // TILE, step, 0)
        send_pieces(src, fr.at[q], f_send.at[q], f_recv.at[q])

    loads[1].wait()
    send_acts(0)

    loads[2].wait()
    wait_pieces(gr, g_sem.at[1])
    expand = one_hot(iota((RANK_ROWS, MARK), 0) >> 6 == iota((RANK_ROWS, MARK), 1))
    marks = gr[:, VALUE:]
    mask_t[...] = dot_t(expand, marks).astype(BF16)
    lift_src[...] = (ADAPTER_SCALE * dot_t(gr[:, :VALUE], up_v[...]) * dot_t(marks, expand)).astype(BF16)
    lift_t[...] = jnp.transpose(lift_src[...].astype(F32)).astype(BF16)

    loads[3].wait()

    def send_terms(q):
        dst = rs.at[q]
        js = slices_of(q)
        for n, j in enumerate(js):
            move = spread(q, [j], 0).astype(BF16)
            for b in range(0, ROWS, 128):
                lift_q[n, b : b + 128] = dot(move, lift_src[b : b + 128]).astype(BF16)

        def step(ct, carry):
            cols = pl.ds(pl.multiple_of(ct * TILE, TILE), TILE)
            total = None
            for n, j in enumerate(js):
                mine = pl.ds(pl.multiple_of(j * SLICE + ct * TILE, TILE), TILE)
                term = dot(lift_q[n], down_v[:, mine])
                total = term if total is None else total + term
            dst[:, cols] = total.astype(BF16)
            return carry

        lax.fori_loop(0, SLICE // TILE, step, 0)
        send_pieces(dst, rr.at[q], r_send.at[q], r_recv.at[q])

    send_terms(0)
    send_terms(1)

    loads[4].wait()
    loads[5].wait()
    pltpu.make_async_copy(wy.at[pl.ds(0, 3)], wy.at[pl.ds(0, 3)], wy_sem.at[1]).wait()
    pltpu.make_async_copy(gx.at[pl.ds(0, 7)], gx.at[pl.ds(0, 7)], gx_sem.at[1]).wait()

    def frozen_step(k, carry):
        half, yy = k // 4, k % 4
        lhs = gx[pl.ds(half * 4, 4)].reshape(4 * TOKENS, VALUE)
        res = dot_t(lhs, wy[yy]).astype(BF16).reshape(4, TOKENS, 256)
        ft[pl.ds(half * 4, 4), :, pl.ds(pl.multiple_of(yy * 256, 256), 256)] = res
        return carry

    lax.fori_loop(0, 8, frozen_step, 0)
    fp[col8] = ft[col8]

    def send_tiles(k, carry):
        other = (col8 + k) % 8
        pltpu.make_async_remote_copy(
            src_ref=ft.at[other], dst_ref=fp.at[col8], send_sem=fp_sem.at[0], recv_sem=fp_sem.at[1],
            device_id=(seg, y * 8 + other), device_id_type=MESH,
        ).start()
        return carry

    lax.fori_loop(1, 8, send_tiles, 0)

    for q in range(2, CHUNKS):
        send_terms(q)
    for q in range(1, CHUNKS):
        send_acts(q)

    low_t[...] = jnp.zeros_like(low_t)

    def out_copy(j):
        cols = pl.ds(j * SLICE, SLICE)
        return pltpu.make_async_copy(dg.at[j % 4], down_grad.at[:, cols], dg_sem.at[j])

    def take_acts(q):
        js = slices_of(q)
        wait_pieces(fr.at[q], f_recv.at[q])
        for n, j in enumerate(js):
            move = spread(q, [j], 1).astype(BF16)
            for b in range(0, ROWS, 128):
                liftt_q[n, :, b : b + 128] = dot(lift_t[:, b : b + 128], move).astype(BF16)
            if first_chunk(j) == q and j >= 4:
                out_copy(j - 4).wait()
        low_q[...] = jnp.zeros_like(low_q)

        def step(ct, carry):
            cols = pl.ds(pl.multiple_of(ct * TILE, TILE), TILE)
            block = fr[q, :, cols]
            total = low_q[...]
            for n, j in enumerate(js):
                mine = pl.ds(pl.multiple_of(j * SLICE + ct * TILE, TILE), TILE)
                rank_at = (iota((RANK_ROWS, ROWS), 1) & 15) + (PIECE * q - CAP * j)
                total += jnp.where((rank_at >= 0) & (rank_at < CAP), dot_t(down_v[:, mine], block), 0.0)
                term = dot(liftt_q[n], block)
                if first_chunk(j) != q:
                    term += dg[j % 4, :, cols]
                dg[j % 4, :, cols] = term
            low_q[...] = total
            return carry

        lax.fori_loop(0, SLICE // TILE, step, 0)
        back = spread(q, js, 0)
        for b in range(0, ROWS, 128):
            low_t[:, b : b + 128] += dot(low_q[:, b : b + 128], back, lax.Precision.HIGHEST)
        for j in js:
            if last_chunk(j) == q:
                out_copy(j).start()

    def hand_on(j):
        cols = pl.ds(j * SLICE, SLICE)
        return pltpu.make_async_remote_copy(
            src_ref=fin.at[:, cols], dst_ref=passed.at[:, cols], send_sem=z_send.at[j], recv_sem=z_recv.at[j],
            device_id=(before, me), device_id_type=MESH,
        )

    def take_terms(q):
        js = slices_of(q)
        wait_pieces(rr.at[q], r_recv.at[q])

        def step(ct, carry):
            cols = pl.ds(pl.multiple_of(ct * TILE, TILE), TILE)
            block = rr[q, :, cols]
            for j in js:
                dest = jnp.concatenate([dest_col[...]] * (ROWS // 128), axis=1)
                term = dot(pick(q, j, 1, dest), block)
                if first_chunk(j) != q:
                    term += pend[:, cols].astype(F32)
                if last_chunk(j) != q:
                    pend[:, cols] = term.astype(BF16)
                else:
                    part = fp[4 * (j % 2) + ct, :, (j // 2) * 256 : (j // 2) * 256 + 256]
                    mine = pl.ds(pl.multiple_of(j * SLICE + ct * TILE, TILE), TILE)
                    fin[:, mine] = (part.astype(F32) + term.astype(BF16).astype(F32)).astype(BF16)
            return carry

        lax.fori_loop(0, SLICE // TILE, step, 0)
        for j in js:
            if last_chunk(j) == q:
                hand_on(j).start()

    take_acts(0)
    pltpu.make_async_copy(fp.at[pl.ds(0, 7)], fp.at[pl.ds(0, 7)], fp_sem.at[1]).wait()
    for q in range(CHUNKS):
        take_terms(q)
    for q in range(1, CHUNKS):
        take_acts(q)

    low_b = (low_t[...] * mask_t[...].astype(F32)).astype(BF16)
    for c0 in range(0, VALUE, TILE):
        ug[:, c0 : c0 + TILE] = ADAPTER_SCALE * dot(low_b, gr[:, c0 : c0 + TILE])
    up_copy = pltpu.make_async_copy(ug, up_grad, ug_sem.at[0])
    up_copy.start()

    wait_pieces(gs, g_sem.at[0])
    pltpu.make_async_copy(wy.at[pl.ds(0, 3)], wy.at[pl.ds(0, 3)], wy_sem.at[0]).wait()
    pltpu.make_async_copy(gx.at[pl.ds(0, 7)], gx.at[pl.ds(0, 7)], gx_sem.at[0]).wait()
    pltpu.make_async_copy(ft.at[pl.ds(0, 7)], ft.at[pl.ds(0, 7)], fp_sem.at[0]).wait()
    for q in range(CHUNKS):
        wait_pieces(fs.at[q], f_send.at[q])
        wait_pieces(rs.at[q], r_send.at[q])
    for j in range(SLICES):
        hand_on(j).wait()
    for j in range(SLICES - 4, SLICES):
        out_copy(j).wait()
    up_copy.wait()


def on_device(acts, output_gradient, frozen, adapter_down, adapter_up, assign, adapter_slot):
    hbm = pl.BlockSpec(memory_space=pl.ANY)
    vmem = pl.BlockSpec(memory_space=pltpu.VMEM)
    dma = pltpu.SemaphoreType.DMA
    passed, down_grad, up_grad = pl.pallas_call(
        kernel,
        out_shape=(
            jax.ShapeDtypeStruct((TOKENS, WIDTH), BF16),
            jax.ShapeDtypeStruct((RANK_ROWS, WIDTH), F32),
            jax.ShapeDtypeStruct((RANK_ROWS, VALUE), F32),
        ),
        in_specs=[hbm] * 5 + [vmem] * 2,
        out_specs=[hbm] * 3,
        scratch_shapes=[
            pltpu.VMEM((TOKENS, WIDTH), BF16),
            pltpu.VMEM((TOKENS, VALUE), BF16),
            pltpu.VMEM((RANK_ROWS, WIDTH), BF16),
            pltpu.VMEM((RANK_ROWS, VALUE), BF16),
            pltpu.VMEM((8, TOKENS), jnp.int32),
            pltpu.VMEM((TOKENS, TOKENS), jnp.int32),
            pltpu.VMEM((ROWS, VALUE + MARK), BF16),
            pltpu.VMEM((ROWS, VALUE + MARK), BF16),
            pltpu.VMEM((CHUNKS, ROWS, SLICE), BF16),
            pltpu.VMEM((CHUNKS, ROWS, SLICE), BF16),
            pltpu.VMEM((CHUNKS, ROWS, SLICE), BF16),
            pltpu.VMEM((CHUNKS, ROWS, SLICE), BF16),
            pltpu.VMEM((8, TOKENS, VALUE), BF16),
            pltpu.VMEM((4, 256, VALUE), BF16),
            pltpu.VMEM((8, TOKENS, 1024), BF16),
            pltpu.VMEM((8, TOKENS, 1024), BF16),
            pltpu.VMEM((ROWS, RANK_ROWS), BF16),
            pltpu.VMEM((RANK_ROWS, ROWS), BF16),
            pltpu.VMEM((RANK_ROWS, ROWS), BF16),
            pltpu.VMEM((3, ROWS, RANK_ROWS), BF16),
            pltpu.VMEM((3, RANK_ROWS, ROWS), BF16),
            pltpu.VMEM((RANK_ROWS, ROWS), F32),
            pltpu.VMEM((RANK_ROWS, ROWS), F32),
            pltpu.VMEM((TOKENS, SLICE), BF16),
            pltpu.VMEM((TOKENS, WIDTH), BF16),
            pltpu.VMEM((4, RANK_ROWS, SLICE), F32),
            pltpu.VMEM((RANK_ROWS, VALUE), F32),
            dma((6,)),
            dma((2,)),
            dma((CHUNKS,)),
            dma((CHUNKS,)),
            dma((CHUNKS,)),
            dma((CHUNKS,)),
            dma((2,)),
            dma((2,)),
            dma((2,)),
            dma((SLICES,)),
            dma((SLICES,)),
            dma((SLICES,)),
            dma((1,)),
        ],
        compiler_params=pltpu.CompilerParams(
            collective_id=0, has_side_effects=True, vmem_limit_bytes=60 * 2**20
        ),
        cost_estimate=pl.CostEstimate(flops=16 * 10**9, bytes_accessed=20 * 2**20, transcendentals=0),
        name="section_backward",
    )(
        acts[0],
        output_gradient[0],
        frozen[0],
        adapter_down.reshape(RANK_ROWS, WIDTH),
        adapter_up.reshape(RANK_ROWS, VALUE),
        assign,
        adapter_slot.reshape(1, -1),
    )
    return (
        passed[None],
        down_grad.reshape(1, 4, 64, WIDTH),
        up_grad.reshape(1, 4, 64, VALUE),
    )


def solution(mesh):
    tok = P("segment", "tok", None)
    mats = P("segment", "tok", None, None)
    return jax.shard_map(
        on_device,
        mesh=mesh,
        in_specs=(tok, tok, tok, mats, mats, P("segment", "tok"), P()),
        out_specs=(tok, mats, mats),
        check_vma=False,
    )
```

```python
import functools

import jax
import jax.numpy as jnp
from jax import lax
from jax.experimental import pallas as pl
from jax.experimental.pallas import tpu as pltpu
from jax.sharding import PartitionSpec as P

MESH = pl.DeviceIdType.MESH
BF16 = jnp.bfloat16
F32 = jnp.float32
ADAPTER_SCALE = 2.0

TOKENS = 128
WIDTH = 8192
VALUE = 1024
RANK_ROWS = 256
OWNERS = 32
CAP = 10
SLICES = 8
SLICE = WIDTH // SLICES
PIECE = 16
CHUNKS = SLICES * CAP // PIECE
ROWS = OWNERS * PIECE
TILE = 256
MARK = 128
NX = 4


def slices_of(chunk):
    first, last = chunk * PIECE // CAP, (chunk * PIECE + PIECE - 1) // CAP
    return list(range(first, last + 1))


def first_chunk(j):
    return j * CAP // PIECE


def last_chunk(j):
    return (j * CAP + CAP - 1) // PIECE


def iota(shape, axis):
    return lax.broadcasted_iota(jnp.int32, shape, axis)


def dot(a, b, precision=None):
    return lax.dot_general(a, b, (((1,), (0,)), ((), ())), precision=precision, preferred_element_type=F32)


def dot_t(a, b):
    return lax.dot_general(a, b, (((1,), (1,)), ((), ())), preferred_element_type=F32)


def one_hot(flag):
    return jnp.where(flag, 1.0, 0.0).astype(BF16)


def pick(chunk, j, axis, dest):
    shape = (ROWS, TOKENS) if axis == 0 else (TOKENS, ROWS)
    row = iota(shape, axis)
    rank = (row & 15) + (PIECE * chunk - CAP * j)
    target = (row >> 4) * CAP + rank
    return one_hot((dest == target) & (rank >= 0) & (rank < CAP))


def spread(chunk, js, axis):
    shape = (128, 128)
    row, col = iota(shape, axis), iota(shape, 1 - axis)
    out = None
    for j in js:
        rank = (row & 15) + (PIECE * chunk - CAP * j)
        flag = ((row >> 4) == (col >> 4)) & ((col & 15) == rank) & (rank >= 0) & (rank < CAP)
        out = flag if out is None else out | flag
    return jnp.where(out, 1.0, 0.0)


def kernel(
    acts, grads, frozen, down, up, assign, slots,
    passed, down_grad, up_grad,
    acts_v, down_v, up_v, dest_row, dest_col,
    info, gs, gd, gr, fs, fr, rs, rr, gx, wy, ft, fp,
    lift_src, lift_t, mask_t, lift_q, liftt_q, low_q, low_t, pend, fin, dg, ug,
    in_sem, info_sem, g_sem, f_send, f_recv, r_send, r_recv, gx_sem, wy_sem, fp_sem, z_send, z_recv, dg_sem, ug_sem,
):
    seg = lax.axis_index("segment")
    me = lax.axis_index("tok")
    y, x, core = me // 8, (me // 2) % 4, me % 2
    col8 = me % 8
    before, after = (seg + 3) % 4, (seg + 1) % 4
    partner = y * 8 + x * 2 + (1 - core)

    loads = [
        pltpu.make_async_copy(grads, gx.at[col8], in_sem.at[0]),
        pltpu.make_async_copy(acts, acts_v, in_sem.at[1]),
        pltpu.make_async_copy(up, up_v, in_sem.at[2]),
        pltpu.make_async_copy(down, down_v, in_sem.at[3]),
        pltpu.make_async_copy(frozen, wy.at[y], in_sem.at[4]),
    ]
    for load in loads:
        load.start()

    barrier = pltpu.get_barrier_semaphore()

    def greet(k, carry):
        pl.semaphore_signal(barrier, inc=1, device_id=(seg, (me + k) % OWNERS), device_id_type=MESH)
        return carry

    lax.fori_loop(1, OWNERS, greet, 0)
    pl.semaphore_signal(barrier, inc=1, device_id=(after, me), device_id_type=MESH)

    match = one_hot(assign[...] == iota((128, 128), 0))
    slot = dot(jnp.broadcast_to(slots[...], (16, 128)).astype(F32).astype(BF16), match)[0:1].astype(jnp.int32)
    owner, local = slot >> 2, slot & 3
    hot = jnp.where(owner == iota((OWNERS, TOKENS), 0), 1.0, 0.0)
    earlier = one_hot(iota((TOKENS, TOKENS), 0) < iota((TOKENS, TOKENS), 1))
    rank = jnp.sum(hot * dot(hot.astype(BF16), earlier), axis=0, keepdims=True)
    dest = owner * CAP + rank.astype(jnp.int32)
    dest_row[...] = jnp.where(iota((8, TOKENS), 0) == 0, dest, local)
    info[col8] = dest_row[...]
    dest_col[...] = jnp.transpose(jnp.broadcast_to(dest.astype(F32), (TOKENS, TOKENS))).astype(jnp.int32)

    def piece(owner_at):
        return pl.ds(pl.multiple_of(owner_at * PIECE, PIECE), PIECE)

    def remote(src, dst, send_sem, recv_sem, to):
        return pltpu.make_async_remote_copy(
            src_ref=src, dst_ref=dst, send_sem=send_sem, recv_sem=recv_sem,
            device_id=(seg, to), device_id_type=MESH,
        )

    def send_act(q, to):
        remote(fs.at[q, piece(to)], fr.at[q, piece(me)], f_send.at[q], f_recv.at[q], to).start()

    def send_term(q, to):
        remote(rs.at[q, piece(to)], rr.at[q, piece(me)], r_send.at[q], r_recv.at[q], to).start()

    def to_x(send, q, side):
        for k in range(1, 4):
            send(q, y * 8 + ((x + k) % 4) * 2 + side)

    def to_y(send, q, side):
        for k in range(1, 4):
            send(q, ((y + k) % 4) * 8 + x * 2 + side)

    def to_rest(send, q):
        def one(n, carry):
            ky, kx, side = n // 6 + 1, (n // 2) % 3 + 1, n % 2
            send(q, ((y + ky) % 4) * 8 + ((x + kx) % 4) * 2 + side)
            return carry

        lax.fori_loop(0, 18, one, 0)
        send(q, partner)

    def wait_pieces(buf, sem):
        others = buf.at[pl.ds(0, ROWS - PIECE)]
        pltpu.make_async_copy(others, others, sem).wait()

    def wait_blocks(buf, count, sem):
        blocks = buf.at[pl.ds(0, count)]
        pltpu.make_async_copy(blocks, blocks, sem).wait()

    pl.semaphore_wait(barrier, OWNERS)

    def send_info(k, carry):
        remote(dest_row, info.at[col8], info_sem.at[0], info_sem.at[1], y * 8 + (col8 + k) % 8).start()
        return carry

    def send_frozen(part, carry):
        at = piece(part)
        for k in range(1, 4):
            to = ((y + k) % 4) * 8 + col8
            remote(frozen.at[at], wy.at[y, at], wy_sem.at[0], wy_sem.at[1], to).start()
        return carry

    def send_grads(part, carry):
        at = piece(part)
        for k in range(1, 4):
            to = y * 8 + (col8 + 2 * k) % 8
            remote(grads.at[at], gx.at[col8, at], gx_sem.at[0], gx_sem.at[1], to).start()
        send_frozen(part, 0)
        return carry

    lax.fori_loop(1, 8, send_info, 0)
    lax.fori_loop(0, TOKENS // PIECE, send_grads, 0)
    remote(grads, gx.at[col8], gx_sem.at[2], gx_sem.at[3], partner).start()

    def pack_acts(q):
        src = fs.at[q]

        def step(ct, carry):
            cols = pl.ds(pl.multiple_of(ct * TILE, TILE), TILE)
            total = None
            for j in slices_of(q):
                mine = pl.ds(pl.multiple_of(j * SLICE + ct * TILE, TILE), TILE)
                term = dot(pick(q, j, 0, dest_row[0:1]), acts_v[:, mine])
                total = term if total is None else total + term
            src[:, cols] = total.astype(BF16)
            return carry

        lax.fori_loop(0, SLICE // TILE, step, 0)
        fr[q, piece(me)] = fs[q, piece(me)]

    loads[1].wait()
    pack_acts(0)
    to_rest(send_act, 0)
    pack_acts(1)
    wait_blocks(gx, 3, gx_sem.at[1])

    def pass_grads(k, carry):
        other = (col8 + 2 * k) % 8
        remote(gx.at[other], gx.at[other], gx_sem.at[2], gx_sem.at[3], partner).start()
        return carry

    lax.fori_loop(1, 4, pass_grads, 0)
    to_rest(send_act, 1)
    pack_acts(2)

    loads[0].wait()
    wait_blocks(info, 7, info_sem.at[1])
    wait_blocks(gx, 4, gx_sem.at[3])
    dest_all = jnp.concatenate([info[k, 0:1] for k in range(8)], axis=1)
    local_all = jnp.concatenate([info[k, 1:2] for k in range(8)], axis=1)
    local_hot = one_hot(local_all == iota((MARK, 8 * TOKENS), 0))
    wanted = (4 * 8 * CAP, 8 * TOKENS)
    at_row = iota(wanted, 0)
    target_y = (at_row >= 80).astype(jnp.int32) + (at_row >= 160).astype(jnp.int32) + (at_row >= 240).astype(jnp.int32)
    within = at_row - 80 * target_y
    source = (within * 205) >> 11
    spot = (target_y * 8 + col8) * CAP + within - CAP * source
    chosen = one_hot((dest_all == spot) & (source == (iota(wanted, 1) >> 7)))
    gs[:, :, VALUE:] = dot_t(chosen, local_hot).astype(BF16).reshape(4, 8 * CAP, MARK)
    for c0 in range(0, VALUE, TILE):
        part = gx[:, :, c0 : c0 + TILE].reshape(8 * TOKENS, TILE)
        gs[:, :, c0 : c0 + TILE] = dot(chosen, part).astype(BF16).reshape(4, 8 * CAP, TILE)
    gd[y] = gs[y]

    def send_rows(part, carry):
        at = piece(part)
        for k in range(1, 4):
            other = (y + k) % 4
            remote(gs.at[other, at], gd.at[y, at], g_sem.at[0], g_sem.at[1], other * 8 + col8).start()
        to_x(send_act, part // 2, part % 2)
        return carry

    lax.fori_loop(0, 8 * CAP // PIECE, send_rows, 0)
    to_x(send_act, 2, 1)
    to_rest(send_act, 2)
    pack_acts(3)
    to_rest(send_act, 3)
    pack_acts(4)

    loads[2].wait()
    wait_blocks(gd, 3, g_sem.at[1])
    row, col = iota((8 * PIECE, 8 * CAP), 0), iota((8 * PIECE, 8 * CAP), 1)
    place = one_hot((col == (row >> 4) * CAP + (row & 15)) & ((row & 15) < CAP))
    for yy in range(4):
        gr[yy * 128 : yy * 128 + 128] = dot(place, gd[yy]).astype(BF16)
    expand = one_hot(iota((RANK_ROWS, MARK), 0) >> 6 == iota((RANK_ROWS, MARK), 1))
    marks = gr[:, VALUE:]
    lifted = (ADAPTER_SCALE * dot_t(gr[:, :VALUE], up_v[...]) * dot_t(marks, expand)).astype(BF16)
    for b in range(4):
        lift_src[:, b * RANK_ROWS : (b + 1) * RANK_ROWS] = lifted[b * 128 : b * 128 + 128]

    loads[3].wait()

    def make_terms(q):
        dst = rs.at[q]
        js = slices_of(q)
        for n, j in enumerate(js):
            moved = dot(spread(q, [j], 0).astype(BF16), lift_src[...]).astype(BF16)
            for b in range(4):
                lift_q[n, b * 128 : b * 128 + 128] = moved[:, b * RANK_ROWS : (b + 1) * RANK_ROWS]

        def step(ct, carry):
            cols = pl.ds(pl.multiple_of(ct * TILE, TILE), TILE)
            total = None
            for n, j in enumerate(js):
                mine = pl.ds(pl.multiple_of(j * SLICE + ct * TILE, TILE), TILE)
                term = dot(lift_q[n], down_v[:, mine])
                total = term if total is None else total + term
            dst[:, cols] = total.astype(BF16)
            return carry

        lax.fori_loop(0, SLICE // TILE, step, 0)
        rr[q, piece(me)] = rs[q, piece(me)]

    make_terms(0)
    make_terms(1)

    def send_frozen_acts(n, carry):
        send_frozen(8 + n, 0)
        to_x(send_act, 3 + n // 2, n % 2)
        return carry

    def send_frozen_terms(n, carry):
        send_frozen(12 + n, 0)
        to_x(send_term, n // 2, n % 2)
        return carry

    lax.fori_loop(0, 4, send_frozen_acts, 0)
    lax.fori_loop(0, 4, send_frozen_terms, 0)
    to_rest(send_term, 0)
    to_rest(send_term, 1)
    make_terms(2)

    loads[4].wait()
    wait_blocks(wy, 3, wy_sem.at[1])

    def frozen_step(k, carry):
        half, yy = k // 4, k % 4
        lhs = gx[pl.ds(half * 4, 4)].reshape(4 * TOKENS, VALUE)
        res = dot_t(lhs, wy[yy]).astype(BF16).reshape(4, TOKENS, 256)
        ft[pl.ds(half * 4, 4), :, pl.ds(pl.multiple_of(yy * 256, 256), 256)] = res
        return carry

    lax.fori_loop(0, 8, frozen_step, 0)
    fp[col8] = ft[col8]

    def send_tiles(part):
        at = piece(part)
        for k in range(1, 8):
            other = (col8 + k) % 8
            remote(ft.at[other, at], fp.at[col8, at], fp_sem.at[0], fp_sem.at[1], y * 8 + other).start()

    def send_tiles_acts(n, carry):
        send_tiles(n)
        to_y(send_act, n, 0)
        to_y(send_act, n, 1)
        return carry

    def send_tiles_terms(n, carry):
        send_tiles(CHUNKS + n)
        to_y(send_term, n, 0)
        to_y(send_term, n, 1)
        return carry

    lax.fori_loop(0, CHUNKS, send_tiles_acts, 0)
    lax.fori_loop(0, TOKENS // PIECE - CHUNKS, send_tiles_terms, 0)

    def send_lines(q, carry):
        to_x(send_term, q, 0)
        to_x(send_term, q, 1)
        return carry

    def send_columns(q, carry):
        to_y(send_term, q, 0)
        to_y(send_term, q, 1)
        return carry

    send_lines(2, 0)
    to_rest(send_term, 2)
    for q in range(3, CHUNKS):
        make_terms(q)
        send_lines(q, 0)
        send_columns(q, 0)
        to_rest(send_term, q)
    to_rest(send_act, 4)

    low_t[...] = jnp.zeros_like(low_t)
    mask_t[...] = dot_t(expand, gr[:, VALUE:]).astype(BF16)
    for b in range(4):
        block = lift_src[:, b * RANK_ROWS : (b + 1) * RANK_ROWS].astype(F32)
        lift_t[:, b * 128 : b * 128 + 128] = jnp.transpose(block).astype(BF16)

    def out_copy(j):
        cols = pl.ds(j * SLICE, SLICE)
        return pltpu.make_async_copy(dg.at[j % 4], down_grad.at[:, cols], dg_sem.at[j])

    def take_acts(q):
        js = slices_of(q)
        wait_pieces(fr.at[q], f_recv.at[q])
        for n, j in enumerate(js):
            move = spread(q, [j], 1).astype(BF16)
            for b in range(0, ROWS, 128):
                liftt_q[n, :, b : b + 128] = dot(lift_t[:, b : b + 128], move).astype(BF16)
            if first_chunk(j) == q and j >= 4:
                out_copy(j - 4).wait()
        low_q[...] = jnp.zeros_like(low_q)

        def step(ct, carry):
            cols = pl.ds(pl.multiple_of(ct * TILE, TILE), TILE)
            block = fr[q, :, cols]
            total = low_q[...]
            for n, j in enumerate(js):
                mine = pl.ds(pl.multiple_of(j * SLICE + ct * TILE, TILE), TILE)
                rank_at = (iota((RANK_ROWS, ROWS), 1) & 15) + (PIECE * q - CAP * j)
                total += jnp.where((rank_at >= 0) & (rank_at < CAP), dot_t(down_v[:, mine], block), 0.0)
                term = dot(liftt_q[n], block)
                if first_chunk(j) != q:
                    term += dg[j % 4, :, cols]
                dg[j % 4, :, cols] = term
            low_q[...] = total
            return carry

        lax.fori_loop(0, SLICE // TILE, step, 0)
        back = spread(q, js, 0)
        for b in range(0, ROWS, 128):
            low_t[:, b : b + 128] += dot(low_q[:, b : b + 128], back, lax.Precision.HIGHEST)
        for j in js:
            if last_chunk(j) == q:
                out_copy(j).start()

    def hand_on(j):
        cols = pl.ds(j * SLICE, SLICE)
        return pltpu.make_async_remote_copy(
            src_ref=fin.at[:, cols], dst_ref=passed.at[:, cols], send_sem=z_send.at[j], recv_sem=z_recv.at[j],
            device_id=(before, me), device_id_type=MESH,
        )

    def take_terms(q):
        js = slices_of(q)
        wait_pieces(rr.at[q], r_recv.at[q])

        def step(ct, carry):
            cols = pl.ds(pl.multiple_of(ct * TILE, TILE), TILE)
            block = rr[q, :, cols]
            for j in js:
                dest = jnp.concatenate([dest_col[...]] * (ROWS // 128), axis=1)
                term = dot(pick(q, j, 1, dest), block)
                if first_chunk(j) != q:
                    term += pend[:, cols].astype(F32)
                if last_chunk(j) != q:
                    pend[:, cols] = term.astype(BF16)
                else:
                    part = fp[4 * (j % 2) + ct, :, (j // 2) * 256 : (j // 2) * 256 + 256]
                    mine = pl.ds(pl.multiple_of(j * SLICE + ct * TILE, TILE), TILE)
                    fin[:, mine] = (part.astype(F32) + term.astype(BF16).astype(F32)).astype(BF16)
            return carry

        lax.fori_loop(0, SLICE // TILE, step, 0)
        for j in js:
            if last_chunk(j) == q:
                hand_on(j).start()

    wait_blocks(fp, 7, fp_sem.at[1])
    take_terms(0)
    take_terms(1)
    take_acts(0)
    take_terms(2)
    take_acts(1)
    take_terms(3)
    take_acts(2)
    take_acts(3)
    take_terms(4)
    take_acts(4)

    low_b = (low_t[...] * mask_t[...].astype(F32)).astype(BF16)
    for c0 in range(0, VALUE, TILE):
        ug[:, c0 : c0 + TILE] = ADAPTER_SCALE * dot(low_b, gr[:, c0 : c0 + TILE])
    up_copy = pltpu.make_async_copy(ug, up_grad, ug_sem.at[0])
    up_copy.start()

    wait_blocks(info, 7, info_sem.at[0])
    wait_blocks(gs, 3, g_sem.at[0])
    wait_blocks(wy, 3, wy_sem.at[0])
    wait_blocks(gx, 3, gx_sem.at[0])
    wait_blocks(gx, 4, gx_sem.at[2])
    wait_blocks(ft, 7, fp_sem.at[0])
    for q in range(CHUNKS):
        wait_pieces(fs.at[q], f_send.at[q])
        wait_pieces(rs.at[q], r_send.at[q])
    for j in range(SLICES):
        hand_on(j).wait()
    for j in range(SLICES - 4, SLICES):
        out_copy(j).wait()
    up_copy.wait()


def on_device(acts, output_gradient, frozen, adapter_down, adapter_up, assign, adapter_slot):
    hbm = pl.BlockSpec(memory_space=pl.ANY)
    vmem = pl.BlockSpec(memory_space=pltpu.VMEM)
    dma = pltpu.SemaphoreType.DMA
    passed, down_grad, up_grad = pl.pallas_call(
        kernel,
        out_shape=(
            jax.ShapeDtypeStruct((TOKENS, WIDTH), BF16),
            jax.ShapeDtypeStruct((RANK_ROWS, WIDTH), F32),
            jax.ShapeDtypeStruct((RANK_ROWS, VALUE), F32),
        ),
        in_specs=[hbm] * 5 + [vmem] * 2,
        out_specs=[hbm] * 3,
        scratch_shapes=[
            pltpu.VMEM((TOKENS, WIDTH), BF16),
            pltpu.VMEM((RANK_ROWS, WIDTH), BF16),
            pltpu.VMEM((RANK_ROWS, VALUE), BF16),
            pltpu.VMEM((8, TOKENS), jnp.int32),
            pltpu.VMEM((TOKENS, TOKENS), jnp.int32),
            pltpu.VMEM((8, 8, TOKENS), jnp.int32),
            pltpu.VMEM((4, 8 * CAP, VALUE + MARK), BF16),
            pltpu.VMEM((4, 8 * CAP, VALUE + MARK), BF16),
            pltpu.VMEM((ROWS, VALUE + MARK), BF16),
            pltpu.VMEM((CHUNKS, ROWS, SLICE), BF16),
            pltpu.VMEM((CHUNKS, ROWS, SLICE), BF16),
            pltpu.VMEM((CHUNKS, ROWS, SLICE), BF16),
            pltpu.VMEM((CHUNKS, ROWS, SLICE), BF16),
            pltpu.VMEM((8, TOKENS, VALUE), BF16),
            pltpu.VMEM((4, 256, VALUE), BF16),
            pltpu.VMEM((8, TOKENS, 1024), BF16),
            pltpu.VMEM((8, TOKENS, 1024), BF16),
            pltpu.VMEM((128, 4 * RANK_ROWS), BF16),
            pltpu.VMEM((RANK_ROWS, ROWS), BF16),
            pltpu.VMEM((RANK_ROWS, ROWS), BF16),
            pltpu.VMEM((3, ROWS, RANK_ROWS), BF16),
            pltpu.VMEM((3, RANK_ROWS, ROWS), BF16),
            pltpu.VMEM((RANK_ROWS, ROWS), F32),
            pltpu.VMEM((RANK_ROWS, ROWS), F32),
            pltpu.VMEM((TOKENS, SLICE), BF16),
            pltpu.VMEM((TOKENS, WIDTH), BF16),
            pltpu.VMEM((4, RANK_ROWS, SLICE), F32),
            pltpu.VMEM((RANK_ROWS, VALUE), F32),
            dma((5,)),
            dma((2,)),
            dma((2,)),
            dma((CHUNKS,)),
            dma((CHUNKS,)),
            dma((CHUNKS,)),
            dma((CHUNKS,)),
            dma((4,)),
            dma((2,)),
            dma((2,)),
            dma((SLICES,)),
            dma((SLICES,)),
            dma((SLICES,)),
            dma((1,)),
        ],
        compiler_params=pltpu.CompilerParams(
            collective_id=0, has_side_effects=True, vmem_limit_bytes=60 * 2**20
        ),
        cost_estimate=pl.CostEstimate(flops=16 * 10**9, bytes_accessed=20 * 2**20, transcendentals=0),
        name="section_backward",
    )(
        acts[0],
        output_gradient[0],
        frozen[0],
        adapter_down.reshape(RANK_ROWS, WIDTH),
        adapter_up.reshape(RANK_ROWS, VALUE),
        assign,
        adapter_slot.reshape(1, -1),
    )
    return (
        passed[None],
        down_grad.reshape(1, 4, 64, WIDTH),
        up_grad.reshape(1, 4, 64, VALUE),
    )


def solution(mesh):
    tok = P("segment", "tok", None)
    mats = P("segment", "tok", None, None)
    return jax.shard_map(
        on_device,
        mesh=mesh,
        in_specs=(tok, tok, tok, mats, mats, P("segment", "tok"), P()),
        out_specs=(tok, mats, mats),
        check_vma=False,
    )
```

```python
import functools

import jax
import jax.numpy as jnp
from jax import lax
from jax.experimental import pallas as pl
from jax.experimental.pallas import tpu as pltpu
from jax.sharding import PartitionSpec as P

MESH = pl.DeviceIdType.MESH
BF16 = jnp.bfloat16
F32 = jnp.float32
ADAPTER_SCALE = 2.0

TOKENS = 128
WIDTH = 8192
VALUE = 1024
RANK_ROWS = 256
OWNERS = 32
CAP = 10
SLICES = 8
SLICE = WIDTH // SLICES
PIECE = 16
CHUNKS = SLICES * CAP // PIECE
ROWS = OWNERS * PIECE
TILE = 256
MARK = 128
NX = 4


def slices_of(chunk):
    first, last = chunk * PIECE // CAP, (chunk * PIECE + PIECE - 1) // CAP
    return list(range(first, last + 1))


def first_chunk(j):
    return j * CAP // PIECE


def last_chunk(j):
    return (j * CAP + CAP - 1) // PIECE


def iota(shape, axis):
    return lax.broadcasted_iota(jnp.int32, shape, axis)


def dot(a, b, precision=None):
    return lax.dot_general(a, b, (((1,), (0,)), ((), ())), precision=precision, preferred_element_type=F32)


def dot_t(a, b):
    return lax.dot_general(a, b, (((1,), (1,)), ((), ())), preferred_element_type=F32)


def one_hot(flag):
    return jnp.where(flag, 1.0, 0.0).astype(BF16)


def pick(chunk, j, axis, dest):
    shape = (ROWS, TOKENS) if axis == 0 else (TOKENS, ROWS)
    row = iota(shape, axis)
    rank = (row & 15) + (PIECE * chunk - CAP * j)
    target = (row >> 4) * CAP + rank
    return one_hot((dest == target) & (rank >= 0) & (rank < CAP))


def spread(chunk, js, axis):
    shape = (128, 128)
    row, col = iota(shape, axis), iota(shape, 1 - axis)
    out = None
    for j in js:
        rank = (row & 15) + (PIECE * chunk - CAP * j)
        flag = ((row >> 4) == (col >> 4)) & ((col & 15) == rank) & (rank >= 0) & (rank < CAP)
        out = flag if out is None else out | flag
    return jnp.where(out, 1.0, 0.0)


def kernel(
    acts, grads, frozen, down, up, assign, slots,
    passed, down_grad, up_grad,
    acts_v, down_v, up_v, dest_row, dest_col,
    info, gs, gd, gr, fs, fr, rs, rr, gx, wy, ft, fp,
    lift_src, lift_t, mask_t, lift_q, liftt_q, low_q, low_t, pend, fin, dg, ug,
    in_sem, info_sem, g_sem, f_send, f_recv, r_send, r_recv, gx_sem, wy_sem, fp_sem, z_send, z_recv, dg_sem, ug_sem,
):
    seg = lax.axis_index("segment")
    me = lax.axis_index("tok")
    y, x, core = me // 8, (me // 2) % 4, me % 2
    col8 = me % 8
    before, after = (seg + 3) % 4, (seg + 1) % 4
    partner = y * 8 + x * 2 + (1 - core)

    loads = [
        pltpu.make_async_copy(grads, gx.at[col8], in_sem.at[0]),
        pltpu.make_async_copy(acts, acts_v, in_sem.at[1]),
        pltpu.make_async_copy(up, up_v, in_sem.at[2]),
        pltpu.make_async_copy(down, down_v, in_sem.at[3]),
        pltpu.make_async_copy(frozen, wy.at[y], in_sem.at[4]),
    ]
    for load in loads:
        load.start()

    barrier = pltpu.get_barrier_semaphore()

    def greet(k, carry):
        pl.semaphore_signal(barrier, inc=1, device_id=(seg, (me + k) % OWNERS), device_id_type=MESH)
        return carry

    lax.fori_loop(1, OWNERS, greet, 0)
    pl.semaphore_signal(barrier, inc=1, device_id=(after, me), device_id_type=MESH)

    match = one_hot(assign[...] == iota((128, 128), 0))
    slot = dot(jnp.broadcast_to(slots[...], (16, 128)).astype(F32).astype(BF16), match)[0:1].astype(jnp.int32)
    owner, local = slot >> 2, slot & 3
    hot = jnp.where(owner == iota((OWNERS, TOKENS), 0), 1.0, 0.0)
    earlier = one_hot(iota((TOKENS, TOKENS), 0) < iota((TOKENS, TOKENS), 1))
    rank = jnp.sum(hot * dot(hot.astype(BF16), earlier), axis=0, keepdims=True)
    dest = owner * CAP + rank.astype(jnp.int32)
    dest_row[...] = jnp.where(iota((8, TOKENS), 0) == 0, dest, local)
    info[col8] = dest_row[...]
    dest_col[...] = jnp.transpose(jnp.broadcast_to(dest.astype(F32), (TOKENS, TOKENS))).astype(jnp.int32)

    def piece(owner_at):
        return pl.ds(pl.multiple_of(owner_at * PIECE, PIECE), PIECE)

    def remote(src, dst, send_sem, recv_sem, to):
        return pltpu.make_async_remote_copy(
            src_ref=src, dst_ref=dst, send_sem=send_sem, recv_sem=recv_sem,
            device_id=(seg, to), device_id_type=MESH,
        )

    def send_act(q, to):
        remote(fs.at[q, piece(to)], fr.at[q, piece(me)], f_send.at[q], f_recv.at[q], to).start()

    def send_term(q, to):
        remote(rs.at[q, piece(to)], rr.at[q, piece(me)], r_send.at[q], r_recv.at[q], to).start()

    def to_x(send, q, side):
        for k in range(1, 4):
            send(q, y * 8 + ((x + k) % 4) * 2 + side)

    def to_y(send, q, side):
        for k in range(1, 4):
            send(q, ((y + k) % 4) * 8 + x * 2 + side)

    def to_rest(send, q):
        def one(n, carry):
            ky, kx, side = n // 6 + 1, (n // 2) % 3 + 1, n % 2
            send(q, ((y + ky) % 4) * 8 + ((x + kx) % 4) * 2 + side)
            return carry

        lax.fori_loop(0, 18, one, 0)
        send(q, partner)

    def wait_pieces(buf, sem):
        others = buf.at[pl.ds(0, ROWS - PIECE)]
        pltpu.make_async_copy(others, others, sem).wait()

    def wait_blocks(buf, count, sem):
        blocks = buf.at[pl.ds(0, count)]
        pltpu.make_async_copy(blocks, blocks, sem).wait()

    pl.semaphore_wait(barrier, OWNERS)

    def send_info(k, carry):
        remote(dest_row, info.at[col8], info_sem.at[0], info_sem.at[1], y * 8 + (col8 + k) % 8).start()
        return carry

    def send_frozen(part, carry):
        at = piece(part)
        for k in range(1, 4):
            to = ((y + k) % 4) * 8 + col8
            remote(frozen.at[at], wy.at[y, at], wy_sem.at[0], wy_sem.at[1], to).start()
        return carry

    def send_grads(part, carry):
        at = piece(part)
        for k in range(1, 4):
            to = y * 8 + (col8 + 2 * k) % 8
            remote(grads.at[at], gx.at[col8, at], gx_sem.at[0], gx_sem.at[1], to).start()
        send_frozen(part, 0)
        return carry

    lax.fori_loop(1, 8, send_info, 0)
    lax.fori_loop(0, TOKENS // PIECE, send_grads, 0)
    remote(grads, gx.at[col8], gx_sem.at[2], gx_sem.at[3], partner).start()

    def pack_acts(q):
        src = fs.at[q]

        def step(ct, carry):
            cols = pl.ds(pl.multiple_of(ct * TILE, TILE), TILE)
            total = None
            for j in slices_of(q):
                mine = pl.ds(pl.multiple_of(j * SLICE + ct * TILE, TILE), TILE)
                term = dot(pick(q, j, 0, dest_row[0:1]), acts_v[:, mine])
                total = term if total is None else total + term
            src[:, cols] = total.astype(BF16)
            return carry

        lax.fori_loop(0, SLICE // TILE, step, 0)
        fr[q, piece(me)] = fs[q, piece(me)]

    loads[1].wait()
    pack_acts(0)
    to_rest(send_act, 0)
    pack_acts(1)
    wait_blocks(gx, 3, gx_sem.at[1])

    def pass_grads(k, carry):
        other = (col8 + 2 * k) % 8
        remote(gx.at[other], gx.at[other], gx_sem.at[2], gx_sem.at[3], partner).start()
        return carry

    lax.fori_loop(1, 4, pass_grads, 0)
    to_rest(send_act, 1)
    pack_acts(2)

    loads[0].wait()
    wait_blocks(info, 7, info_sem.at[1])
    wait_blocks(gx, 4, gx_sem.at[3])
    dest_all = jnp.concatenate([info[k, 0:1] for k in range(8)], axis=1)
    local_all = jnp.concatenate([info[k, 1:2] for k in range(8)], axis=1)
    local_hot = one_hot(local_all == iota((MARK, 8 * TOKENS), 0))
    wanted = (4 * 8 * CAP, 8 * TOKENS)
    at_row = iota(wanted, 0)
    target_y = (at_row >= 80).astype(jnp.int32) + (at_row >= 160).astype(jnp.int32) + (at_row >= 240).astype(jnp.int32)
    within = at_row - 80 * target_y
    source = (within * 205) >> 11
    spot = (target_y * 8 + col8) * CAP + within - CAP * source
    chosen = one_hot((dest_all == spot) & (source == (iota(wanted, 1) >> 7)))
    gs[:, :, VALUE:] = dot_t(chosen, local_hot).astype(BF16).reshape(4, 8 * CAP, MARK)
    for c0 in range(0, VALUE, TILE):
        part = gx[:, :, c0 : c0 + TILE].reshape(8 * TOKENS, TILE)
        gs[:, :, c0 : c0 + TILE] = dot(chosen, part).astype(BF16).reshape(4, 8 * CAP, TILE)
    gd[y] = gs[y]

    def send_rows(part, carry):
        at = piece(part)
        for k in range(1, 4):
            other = (y + k) % 4
            remote(gs.at[other, at], gd.at[y, at], g_sem.at[0], g_sem.at[1], other * 8 + col8).start()
        to_x(send_act, part // 2, part % 2)
        return carry

    lax.fori_loop(0, 8 * CAP // PIECE, send_rows, 0)
    to_x(send_act, 2, 1)
    to_rest(send_act, 2)
    pack_acts(3)
    to_rest(send_act, 3)
    pack_acts(4)

    def send_frozen_acts(n, carry):
        send_frozen(8 + n, 0)
        to_x(send_act, 3 + n // 2, n % 2)
        return carry

    lax.fori_loop(0, 4, send_frozen_acts, 0)

    loads[2].wait()
    wait_blocks(gd, 3, g_sem.at[1])
    row, col = iota((8 * PIECE, 8 * CAP), 0), iota((8 * PIECE, 8 * CAP), 1)
    place = one_hot((col == (row >> 4) * CAP + (row & 15)) & ((row & 15) < CAP))
    for yy in range(4):
        gr[yy * 128 : yy * 128 + 128] = dot(place, gd[yy]).astype(BF16)
    expand = one_hot(iota((RANK_ROWS, MARK), 0) >> 6 == iota((RANK_ROWS, MARK), 1))
    marks = gr[:, VALUE:]
    lifted = (ADAPTER_SCALE * dot_t(gr[:, :VALUE], up_v[...]) * dot_t(marks, expand)).astype(BF16)
    for b in range(4):
        lift_src[:, b * RANK_ROWS : (b + 1) * RANK_ROWS] = lifted[b * 128 : b * 128 + 128]

    loads[3].wait()

    def make_terms(q):
        dst = rs.at[q]
        js = slices_of(q)
        for n, j in enumerate(js):
            moved = dot(spread(q, [j], 0).astype(BF16), lift_src[...]).astype(BF16)
            for b in range(4):
                lift_q[n, b * 128 : b * 128 + 128] = moved[:, b * RANK_ROWS : (b + 1) * RANK_ROWS]

        def step(ct, carry):
            cols = pl.ds(pl.multiple_of(ct * TILE, TILE), TILE)
            total = None
            for n, j in enumerate(js):
                mine = pl.ds(pl.multiple_of(j * SLICE + ct * TILE, TILE), TILE)
                term = dot(lift_q[n], down_v[:, mine])
                total = term if total is None else total + term
            dst[:, cols] = total.astype(BF16)
            return carry

        lax.fori_loop(0, SLICE // TILE, step, 0)
        rr[q, piece(me)] = rs[q, piece(me)]

    make_terms(0)
    make_terms(1)

    def send_frozen_terms(n, carry):
        send_frozen(12 + n, 0)
        to_x(send_term, n // 2, n % 2)
        return carry

    lax.fori_loop(0, 4, send_frozen_terms, 0)
    to_rest(send_term, 0)
    to_rest(send_term, 1)
    make_terms(2)

    loads[4].wait()
    wait_blocks(wy, 3, wy_sem.at[1])

    def frozen_step(k, carry):
        half, yy = k // 4, k % 4
        lhs = gx[pl.ds(half * 4, 4)].reshape(4 * TOKENS, VALUE)
        res = dot_t(lhs, wy[yy]).astype(BF16).reshape(4, TOKENS, 256)
        ft[pl.ds(half * 4, 4), :, pl.ds(pl.multiple_of(yy * 256, 256), 256)] = res
        return carry

    lax.fori_loop(0, 8, frozen_step, 0)
    fp[col8] = ft[col8]

    def send_tiles(part):
        at = piece(part)
        for k in range(1, 8):
            other = (col8 + k) % 8
            remote(ft.at[other, at], fp.at[col8, at], fp_sem.at[0], fp_sem.at[1], y * 8 + other).start()

    def send_tiles_acts(n, carry):
        send_tiles(n)
        to_y(send_act, n, 0)
        to_y(send_act, n, 1)
        return carry

    def send_tiles_terms(n, carry):
        send_tiles(CHUNKS + n)
        to_y(send_term, n, 0)
        to_y(send_term, n, 1)
        return carry

    lax.fori_loop(0, CHUNKS, send_tiles_acts, 0)
    lax.fori_loop(0, TOKENS // PIECE - CHUNKS, send_tiles_terms, 0)

    def send_lines(q, carry):
        to_x(send_term, q, 0)
        to_x(send_term, q, 1)
        return carry

    def send_columns(q, carry):
        to_y(send_term, q, 0)
        to_y(send_term, q, 1)
        return carry

    send_lines(2, 0)
    to_rest(send_term, 2)
    for q in range(3, CHUNKS):
        make_terms(q)
        send_lines(q, 0)
        send_columns(q, 0)
        to_rest(send_term, q)
    to_rest(send_act, 4)

    low_t[...] = jnp.zeros_like(low_t)
    mask_t[...] = dot_t(expand, gr[:, VALUE:]).astype(BF16)
    for b in range(4):
        block = lift_src[:, b * RANK_ROWS : (b + 1) * RANK_ROWS].astype(F32)
        lift_t[:, b * 128 : b * 128 + 128] = jnp.transpose(block).astype(BF16)

    def out_copy(j):
        cols = pl.ds(j * SLICE, SLICE)
        return pltpu.make_async_copy(dg.at[j % 4], down_grad.at[:, cols], dg_sem.at[j])

    def take_acts(q):
        js = slices_of(q)
        wait_pieces(fr.at[q], f_recv.at[q])
        for n, j in enumerate(js):
            move = spread(q, [j], 1).astype(BF16)
            for b in range(0, ROWS, 128):
                liftt_q[n, :, b : b + 128] = dot(lift_t[:, b : b + 128], move).astype(BF16)
            if first_chunk(j) == q and j >= 4:
                out_copy(j - 4).wait()
        low_q[...] = jnp.zeros_like(low_q)

        def step(ct, carry):
            cols = pl.ds(pl.multiple_of(ct * TILE, TILE), TILE)
            block = fr[q, :, cols]
            total = low_q[...]
            for n, j in enumerate(js):
                mine = pl.ds(pl.multiple_of(j * SLICE + ct * TILE, TILE), TILE)
                rank_at = (iota((RANK_ROWS, ROWS), 1) & 15) + (PIECE * q - CAP * j)
                total += jnp.where((rank_at >= 0) & (rank_at < CAP), dot_t(down_v[:, mine], block), 0.0)
                term = dot(liftt_q[n], block)
                if first_chunk(j) != q:
                    term += dg[j % 4, :, cols]
                dg[j % 4, :, cols] = term
            low_q[...] = total
            return carry

        lax.fori_loop(0, SLICE // TILE, step, 0)
        back = spread(q, js, 0)
        for b in range(0, ROWS, 128):
            low_t[:, b : b + 128] += dot(low_q[:, b : b + 128], back, lax.Precision.HIGHEST)
        for j in js:
            if last_chunk(j) == q:
                out_copy(j).start()

    def hand_on(j):
        cols = pl.ds(j * SLICE, SLICE)
        return pltpu.make_async_remote_copy(
            src_ref=fin.at[:, cols], dst_ref=passed.at[:, cols], send_sem=z_send.at[j], recv_sem=z_recv.at[j],
            device_id=(before, me), device_id_type=MESH,
        )

    def take_terms(q):
        js = slices_of(q)
        wait_pieces(rr.at[q], r_recv.at[q])

        def step(ct, carry):
            cols = pl.ds(pl.multiple_of(ct * TILE, TILE), TILE)
            block = rr[q, :, cols]
            for j in js:
                dest = jnp.concatenate([dest_col[...]] * (ROWS // 128), axis=1)
                term = dot(pick(q, j, 1, dest), block)
                if first_chunk(j) != q:
                    term += pend[:, cols].astype(F32)
                if last_chunk(j) != q:
                    pend[:, cols] = term.astype(BF16)
                else:
                    part = fp[4 * (j % 2) + ct, :, (j // 2) * 256 : (j // 2) * 256 + 256]
                    mine = pl.ds(pl.multiple_of(j * SLICE + ct * TILE, TILE), TILE)
                    fin[:, mine] = (part.astype(F32) + term.astype(BF16).astype(F32)).astype(BF16)
            return carry

        lax.fori_loop(0, SLICE // TILE, step, 0)
        for j in js:
            if last_chunk(j) == q:
                hand_on(j).start()

    wait_blocks(fp, 7, fp_sem.at[1])
    take_terms(0)
    take_terms(1)
    take_acts(0)
    take_terms(2)
    take_acts(1)
    take_terms(3)
    take_acts(2)
    take_acts(3)
    take_terms(4)
    take_acts(4)

    low_b = (low_t[...] * mask_t[...].astype(F32)).astype(BF16)
    for c0 in range(0, VALUE, TILE):
        ug[:, c0 : c0 + TILE] = ADAPTER_SCALE * dot(low_b, gr[:, c0 : c0 + TILE])
    up_copy = pltpu.make_async_copy(ug, up_grad, ug_sem.at[0])
    up_copy.start()

    wait_blocks(info, 7, info_sem.at[0])
    wait_blocks(gs, 3, g_sem.at[0])
    wait_blocks(wy, 3, wy_sem.at[0])
    wait_blocks(gx, 3, gx_sem.at[0])
    wait_blocks(gx, 4, gx_sem.at[2])
    wait_blocks(ft, 7, fp_sem.at[0])
    for q in range(CHUNKS):
        wait_pieces(fs.at[q], f_send.at[q])
        wait_pieces(rs.at[q], r_send.at[q])
    for j in range(SLICES):
        hand_on(j).wait()
    for j in range(SLICES - 4, SLICES):
        out_copy(j).wait()
    up_copy.wait()


def settle(passed, down_grad, up_grad, passed_out, down_out, up_out, p_v, d_v, u_v, sem, sem_out):
    moves = []
    for src, mid, dst, rows in (
        (down_grad, d_v, down_out, 32), (passed, p_v, passed_out, 64), (up_grad, u_v, up_out, 256),
    ):
        for r0 in range(0, src.shape[0], rows):
            at, n = pl.ds(r0, rows), len(moves)
            moves.append((
                pltpu.make_async_copy(src.at[at], mid.at[at], sem.at[n]),
                pltpu.make_async_copy(mid.at[at], dst.at[at], sem_out.at[n]),
            ))
    for load, _ in moves:
        load.start()
    for load, store in moves:
        load.wait()
        store.start()
    for _, store in moves:
        store.wait()


def on_device(acts, output_gradient, frozen, adapter_down, adapter_up, assign, adapter_slot):
    hbm = pl.BlockSpec(memory_space=pl.ANY)
    vmem = pl.BlockSpec(memory_space=pltpu.VMEM)
    dma = pltpu.SemaphoreType.DMA
    passed, down_grad, up_grad = pl.pallas_call(
        kernel,
        out_shape=(
            jax.ShapeDtypeStruct((TOKENS, WIDTH), BF16),
            jax.ShapeDtypeStruct((RANK_ROWS, WIDTH), F32),
            jax.ShapeDtypeStruct((RANK_ROWS, VALUE), F32),
        ),
        in_specs=[hbm] * 5 + [vmem] * 2,
        out_specs=[hbm] * 3,
        scratch_shapes=[
            pltpu.VMEM((TOKENS, WIDTH), BF16),
            pltpu.VMEM((RANK_ROWS, WIDTH), BF16),
            pltpu.VMEM((RANK_ROWS, VALUE), BF16),
            pltpu.VMEM((8, TOKENS), jnp.int32),
            pltpu.VMEM((TOKENS, TOKENS), jnp.int32),
            pltpu.VMEM((8, 8, TOKENS), jnp.int32),
            pltpu.VMEM((4, 8 * CAP, VALUE + MARK), BF16),
            pltpu.VMEM((4, 8 * CAP, VALUE + MARK), BF16),
            pltpu.VMEM((ROWS, VALUE + MARK), BF16),
            pltpu.VMEM((CHUNKS, ROWS, SLICE), BF16),
            pltpu.VMEM((CHUNKS, ROWS, SLICE), BF16),
            pltpu.VMEM((CHUNKS, ROWS, SLICE), BF16),
            pltpu.VMEM((CHUNKS, ROWS, SLICE), BF16),
            pltpu.VMEM((8, TOKENS, VALUE), BF16),
            pltpu.VMEM((4, 256, VALUE), BF16),
            pltpu.VMEM((8, TOKENS, 1024), BF16),
            pltpu.VMEM((8, TOKENS, 1024), BF16),
            pltpu.VMEM((128, 4 * RANK_ROWS), BF16),
            pltpu.VMEM((RANK_ROWS, ROWS), BF16),
            pltpu.VMEM((RANK_ROWS, ROWS), BF16),
            pltpu.VMEM((3, ROWS, RANK_ROWS), BF16),
            pltpu.VMEM((3, RANK_ROWS, ROWS), BF16),
            pltpu.VMEM((RANK_ROWS, ROWS), F32),
            pltpu.VMEM((RANK_ROWS, ROWS), F32),
            pltpu.VMEM((TOKENS, SLICE), BF16),
            pltpu.VMEM((TOKENS, WIDTH), BF16),
            pltpu.VMEM((4, RANK_ROWS, SLICE), F32),
            pltpu.VMEM((RANK_ROWS, VALUE), F32),
            dma((5,)),
            dma((2,)),
            dma((2,)),
            dma((CHUNKS,)),
            dma((CHUNKS,)),
            dma((CHUNKS,)),
            dma((CHUNKS,)),
            dma((4,)),
            dma((2,)),
            dma((2,)),
            dma((SLICES,)),
            dma((SLICES,)),
            dma((SLICES,)),
            dma((1,)),
        ],
        compiler_params=pltpu.CompilerParams(
            collective_id=0, has_side_effects=True, vmem_limit_bytes=60 * 2**20
        ),
        cost_estimate=pl.CostEstimate(flops=16 * 10**9, bytes_accessed=20 * 2**20, transcendentals=0),
        name="section_backward",
    )(
        acts[0],
        output_gradient[0],
        frozen[0],
        adapter_down.reshape(RANK_ROWS, WIDTH),
        adapter_up.reshape(RANK_ROWS, VALUE),
        assign,
        adapter_slot.reshape(1, -1),
    )
    passed, down_grad, up_grad = pl.pallas_call(
        settle,
        out_shape=(
            jax.ShapeDtypeStruct((TOKENS, WIDTH), BF16),
            jax.ShapeDtypeStruct((RANK_ROWS, WIDTH), F32),
            jax.ShapeDtypeStruct((RANK_ROWS, VALUE), F32),
        ),
        in_specs=[hbm] * 3,
        out_specs=[hbm] * 3,
        scratch_shapes=[
            pltpu.VMEM((TOKENS, WIDTH), BF16),
            pltpu.VMEM((RANK_ROWS, WIDTH), F32),
            pltpu.VMEM((RANK_ROWS, VALUE), F32),
            dma((11,)),
            dma((11,)),
        ],
        compiler_params=pltpu.CompilerParams(vmem_limit_bytes=60 * 2**20),
        name="settle",
    )(passed, down_grad, up_grad)
    return (
        passed[None],
        down_grad.reshape(1, 4, 64, WIDTH),
        up_grad.reshape(1, 4, 64, VALUE),
    )


def solution(mesh):
    tok = P("segment", "tok", None)
    mats = P("segment", "tok", None, None)
    return jax.shard_map(
        on_device,
        mesh=mesh,
        in_specs=(tok, tok, tok, mats, mats, P("segment", "tok"), P()),
        out_specs=(tok, mats, mats),
        check_vma=False,
    )
```
